32 devices in a mesh: dish: 4 (over y, x), blk: 8 (over z, core).
Axes of the slice: x: 2, y: 2, z: 4, core: 2. Of those that a mesh axis runs over, the one named last changes fastest.
Arguments:
- sky_data: float32 [4, 2048, 32768], P('dish', 'blk'), may hold values from -6 to 6
- eigenmodes: float32 [2048, 64], replicated, may hold values from -0.125 to 0.125
- noise_power: float32 [64, 32768], P('blk'), may hold values from 0.1 to 10
Outputs:
- cleaned: bfloat16 [4, 2048, 32768], P('dish', 'blk')
- mode_signal: float32 [4, 64, 32768], P('dish', 'blk')
The draws below stay inside these ranges and needn't reach their ends.
All inputs are finite; a program needn't handle non-finite values.
Results may differ from the reference program's by a relative error of at most 0.0028.
Values may be sent and summed in bfloat16 or wider, within the bound.
A program may use at most 192 MiB of HBM per device.

```python
import math
import jax
import jax.numpy as jnp
from jax import lax

CH = 2048
MODES = 64
NT = 32768
DISHES = 4


def block_levels(key, shape, cuts, low, high):
    level, own = 1.0, jax.random.fold_in(key, 6)
    for axis_at, blocks in cuts:
        heights = jnp.exp(jax.random.uniform(jax.random.fold_in(own, axis_at), (blocks,), jnp.float32, low / len(cuts), high / len(cuts)))
        level = level * jnp.repeat(heights, shape[axis_at] // blocks).reshape([-1 if axis == axis_at else 1 for axis in range(len(shape))])
    return level


def bell_draw(rng, extent, deviation, most, pieces=(), held_as=jnp.bfloat16):
    factor_of = block_levels(rng, extent, pieces, -0.22, 0.18) if pieces else 1.0
    result = jax.random.normal(rng, extent, jnp.float32) * deviation * factor_of
    return jnp.minimum(jnp.maximum(result, -most), most).astype(held_as)


def setup_inputs(seed: int = 0) -> dict:
    key_list = jax.random.split(jax.random.key(seed), 4)
    sky_data = bell_draw(key_list[0], (DISHES, CH, NT), 1.0, 6.0, ((0, 4), (1, 8)), jnp.float32)
    eigenmodes = bell_draw(key_list[1], (CH, MODES), CH ** -0.5, 0.125, (), jnp.float32)
    noise_power = jnp.clip(jnp.exp(math.log(10.0) - 4.6051702 * jax.random.uniform(key_list[2], (MODES, NT), jnp.float32) ** block_levels(key_list[2], (MODES, NT), ((0, 8),), -0.2, 0.2)), 0.1, 10.0)
    return dict(sky_data=sky_data, eigenmodes=eigenmodes, noise_power=noise_power)


def reference(sky_data, eigenmodes, noise_power):
    def project(block):
        return jnp.dot(eigenmodes.T, block, precision=lax.Precision.HIGHEST, preferred_element_type=jnp.float32)

    amplitude = lax.map(project, sky_data)
    spectrum = jnp.fft.fft(amplitude, axis=-1)
    power = jnp.sum(spectrum.real * spectrum.real + spectrum.imag * spectrum.imag, axis=0) / (DISHES * NT)
    gain = power / (power + noise_power)
    mode_signal = jnp.fft.ifft(spectrum * gain[None], axis=-1).real.astype(jnp.float32)

    def remove(pair):
        block, signal = pair
        fitted = jnp.dot(eigenmodes, signal, precision=lax.Precision.HIGHEST, preferred_element_type=jnp.float32)
        return (block - fitted).astype(jnp.bfloat16)

    cleaned = lax.map(remove, (sky_data, mode_signal))
    return cleaned, mode_signal
```

```python
import math

import jax
import jax.numpy as jnp
from jax import lax
from jax.experimental import pallas as pl
from jax.experimental.pallas import tpu as pltpu
from jax.sharding import PartitionSpec as P

highest = lax.Precision.HIGH


def dft_table(length):
    index = jnp.arange(length, dtype=jnp.int32)
    phase = (index[:, None] * index[None, :] % length).astype(jnp.float32) * (
        2.0 * math.pi / length
    )
    return (jnp.cos(phase), jnp.sin(phase))


def twist_table(rows_count, cols_count):
    total = rows_count * cols_count
    first = jnp.arange(rows_count, dtype=jnp.int32)
    second = jnp.arange(cols_count, dtype=jnp.int32)
    phase = (first[:, None] * second[None, :] % total).astype(jnp.float32) * (2.0 * math.pi / total)
    return (jnp.cos(phase), jnp.sin(phase))


def forward(series, tables):
    col_cos, col_sin, row_cos, row_sin, twist_cos, twist_sin = tables
    batch_count, length = series.shape
    grid = series.reshape(batch_count, length // 128, 128)
    inner_real = jnp.einsum("bqp,qk->bpk", grid, col_cos, precision=highest)
    inner_imag = -jnp.einsum("bqp,qk->bpk", grid, col_sin, precision=highest)
    turned_real = inner_real * twist_cos + inner_imag * twist_sin
    turned_imag = inner_imag * twist_cos - inner_real * twist_sin
    spec_real = jnp.einsum("kp,bpj->bkj", row_cos, turned_real, precision=highest) + jnp.einsum(
        "kp,bpj->bkj", row_sin, turned_imag, precision=highest
    )
    spec_imag = jnp.einsum("kp,bpj->bkj", row_cos, turned_imag, precision=highest) - jnp.einsum(
        "kp,bpj->bkj", row_sin, turned_real, precision=highest
    )
    return (spec_real, spec_imag)


def inverse(held_real, held_imag, tables, length):
    col_cos, col_sin, row_cos, row_sin, twist_cos, twist_sin = tables
    outer_real = jnp.einsum("pk,bkj->bpj", row_cos, held_real, precision=highest) - jnp.einsum(
        "pk,bkj->bpj", row_sin, held_imag, precision=highest
    )
    outer_imag = jnp.einsum("pk,bkj->bpj", row_cos, held_imag, precision=highest) + jnp.einsum(
        "pk,bkj->bpj", row_sin, held_real, precision=highest
    )
    back_real = outer_real * twist_cos - outer_imag * twist_sin
    back_imag = outer_real * twist_sin + outer_imag * twist_cos
    series = jnp.einsum("qk,bpk->bqp", col_cos, back_real, precision=highest) - jnp.einsum(
        "qk,bpk->bqp", col_sin, back_imag, precision=highest
    )
    return (series / length).reshape(held_real.shape[0], length)


def wiener(amplitude, noise_power):
    dish_local = amplitude.shape[0]
    owned_modes = amplitude.shape[1]
    length = amplitude.shape[2]
    columns = length // 128
    col_cos, col_sin = dft_table(columns)
    row_cos, row_sin = dft_table(128)
    twist_cos, twist_sin = twist_table(128, columns)
    tables = (col_cos, col_sin, row_cos, row_sin, twist_cos, twist_sin)
    spec_real, spec_imag = forward(amplitude.reshape(dish_local * owned_modes, length), tables)
    squared = spec_real * spec_real + spec_imag * spec_imag
    power_here = jnp.sum(squared.reshape(dish_local, owned_modes, 128, columns), axis=0)
    power_total = lax.psum(power_here.astype(jnp.bfloat16), "dish").astype(jnp.float32)
    power = power_total / float(dish_local * lax.axis_size("dish") * length)
    gain = power / (power + noise_power.reshape(owned_modes, 128, columns))
    gain_rows = gain[None].reshape(dish_local * owned_modes, 128, columns)
    signal = inverse(spec_real * gain_rows, spec_imag * gain_rows, tables, length)
    return signal.reshape(dish_local, owned_modes, length)


def split(value):
    top = value.astype(jnp.bfloat16)
    return top, (value - top.astype(jnp.float32)).astype(jnp.bfloat16)


def project_kernel(modes_ref, sky_ref, out_ref):
    count = out_ref.shape[0]
    top, rest = split(sky_ref[0])
    both = jnp.dot(modes_ref[...], top, preferred_element_type=jnp.float32)
    low = jnp.dot(modes_ref[:count], rest, preferred_element_type=jnp.float32)
    out_ref[...] = (both[:count] + both[count:] + low).astype(out_ref.dtype)


def clean_kernel(modes_ref, sky_ref, signal_ref, out_ref):
    signal = signal_ref[...]
    fitted = jnp.dot(
        modes_ref[...],
        jnp.concatenate([signal, signal], axis=0),
        preferred_element_type=jnp.float32,
    )
    out_ref[0] = (sky_ref[0] - fitted).astype(jnp.bfloat16)


def body(sky_data, eigenmodes, noise_power):
    channels, length = sky_data.shape[1:]
    count = eigenmodes.shape[1]
    width = min(2048, length)
    position = lax.axis_index("blk")
    local_modes = lax.dynamic_slice_in_dim(eigenmodes, position * channels, channels, 0)
    top, rest = split(local_modes)
    wide = jnp.concatenate([top, rest], axis=1)
    partial = pl.pallas_call(
        project_kernel,
        grid=(length // width,),
        in_specs=[
            pl.BlockSpec((2 * count, channels), lambda i: (0, 0)),
            pl.BlockSpec((1, channels, width), lambda i: (0, 0, i)),
        ],
        out_specs=pl.BlockSpec((count, width), lambda i: (0, i)),
        out_shape=jax.ShapeDtypeStruct((count, length), jnp.float32),
        compiler_params=pltpu.CompilerParams(vmem_limit_bytes=40 * 2**20),
    )(wide.T, sky_data)
    summed = lax.psum_scatter(partial, "blk", scatter_dimension=0, tiled=True)
    signal = wiener(summed[None], noise_power)
    everyone = lax.all_gather(signal[0].astype(jnp.bfloat16), "blk", axis=0, tiled=True)
    cleaned = pl.pallas_call(
        clean_kernel,
        grid=(length // width,),
        in_specs=[
            pl.BlockSpec((channels, 2 * count), lambda i: (0, 0)),
            pl.BlockSpec((1, channels, width), lambda i: (0, 0, i)),
            pl.BlockSpec((count, width), lambda i: (0, i)),
        ],
        out_specs=pl.BlockSpec((1, channels, width), lambda i: (0, 0, i)),
        out_shape=jax.ShapeDtypeStruct(sky_data.shape, jnp.bfloat16),
        compiler_params=pltpu.CompilerParams(vmem_limit_bytes=40 * 2**20),
    )(wide, sky_data, everyone)
    return (cleaned, signal)


def solution(mesh):
    return jax.shard_map(
        body,
        mesh=mesh,
        in_specs=(P("dish", "blk", None), P(), P("blk", None)),
        out_specs=(P("dish", "blk", None), P("dish", "blk", None)),
        check_vma=False,
    )
```

```python
import functools
import math

import jax
import jax.numpy as jnp
from jax import lax
from jax.experimental import pallas as pl
from jax.experimental.pallas import tpu as pltpu
from jax.sharding import PartitionSpec as P

highest = lax.Precision.HIGH


def dft_table(length):
    index = jnp.arange(length, dtype=jnp.int32)
    phase = (index[:, None] * index[None, :] % length).astype(jnp.float32) * (
        2.0 * math.pi / length
    )
    return (jnp.cos(phase), jnp.sin(phase))


def twist_table(rows_count, cols_count):
    total = rows_count * cols_count
    first = jnp.arange(rows_count, dtype=jnp.int32)
    second = jnp.arange(cols_count, dtype=jnp.int32)
    phase = (first[:, None] * second[None, :] % total).astype(jnp.float32) * (2.0 * math.pi / total)
    return (jnp.cos(phase), jnp.sin(phase))


def forward(series, tables):
    col_cos, col_sin, row_cos, row_sin, twist_cos, twist_sin = tables
    batch_count, length = series.shape
    grid = series.reshape(batch_count, length // 128, 128)
    inner_real = jnp.einsum("bqp,qk->bpk", grid, col_cos, precision=highest)
    inner_imag = -jnp.einsum("bqp,qk->bpk", grid, col_sin, precision=highest)
    turned_real = inner_real * twist_cos + inner_imag * twist_sin
    turned_imag = inner_imag * twist_cos - inner_real * twist_sin
    spec_real = jnp.einsum("kp,bpj->bkj", row_cos, turned_real, precision=highest) + jnp.einsum(
        "kp,bpj->bkj", row_sin, turned_imag, precision=highest
    )
    spec_imag = jnp.einsum("kp,bpj->bkj", row_cos, turned_imag, precision=highest) - jnp.einsum(
        "kp,bpj->bkj", row_sin, turned_real, precision=highest
    )
    return (spec_real, spec_imag)


def inverse(held_real, held_imag, tables, length):
    col_cos, col_sin, row_cos, row_sin, twist_cos, twist_sin = tables
    outer_real = jnp.einsum("pk,bkj->bpj", row_cos, held_real, precision=highest) - jnp.einsum(
        "pk,bkj->bpj", row_sin, held_imag, precision=highest
    )
    outer_imag = jnp.einsum("pk,bkj->bpj", row_cos, held_imag, precision=highest) + jnp.einsum(
        "pk,bkj->bpj", row_sin, held_real, precision=highest
    )
    back_real = outer_real * twist_cos - outer_imag * twist_sin
    back_imag = outer_real * twist_sin + outer_imag * twist_cos
    series = jnp.einsum("qk,bpk->bqp", col_cos, back_real, precision=highest) - jnp.einsum(
        "qk,bpk->bqp", col_sin, back_imag, precision=highest
    )
    return (series / length).reshape(held_real.shape[0], length)


def wiener(amplitude, noise_power):
    dish_local = amplitude.shape[0]
    owned_modes = amplitude.shape[1]
    length = amplitude.shape[2]
    columns = length // 128
    col_cos, col_sin = dft_table(columns)
    row_cos, row_sin = dft_table(128)
    twist_cos, twist_sin = twist_table(128, columns)
    tables = (col_cos, col_sin, row_cos, row_sin, twist_cos, twist_sin)
    spec_real, spec_imag = forward(amplitude.reshape(dish_local * owned_modes, length), tables)
    squared = spec_real * spec_real + spec_imag * spec_imag
    power_here = jnp.sum(squared.reshape(dish_local, owned_modes, 128, columns), axis=0)
    power_total = sum_over_dishes(power_here)
    power = power_total / float(dish_local * lax.axis_size("dish") * length)
    gain = power / (power + noise_power.reshape(owned_modes, 128, columns))
    gain_rows = gain[None].reshape(dish_local * owned_modes, 128, columns)
    signal = inverse(spec_real * gain_rows, spec_imag * gain_rows, tables, length)
    return signal.reshape(dish_local, owned_modes, length)


def split(value):
    top = value.astype(jnp.bfloat16)
    return top, (value - top.astype(jnp.float32)).astype(jnp.bfloat16)


MESH = pl.DeviceIdType.MESH


def scatter_kernel(
    chips, chunks, wire, modes_ref, sky_ref, out_ref,
    own, give, taken, stage_up, stage_down, from_below, from_above,
    pair_send, pair_recv, up_send, up_recv, down_send, down_recv,
):
    step = pl.program_id(0)
    me = lax.axis_index("blk")
    place = me // 2
    partner = me + 1 - 2 * (me % 2)
    has_below = place > 0
    has_above = place < chips - 1
    half = modes_ref.shape[0] // 4
    count = half // chips
    folded = out_ref.shape[2]
    folds = out_ref.shape[1] // count

    def pair_copy(chunk):
        return pltpu.make_async_remote_copy(
            src_ref=give.at[chunk], dst_ref=taken.at[chunk],
            send_sem=pair_send.at[chunk], recv_sem=pair_recv.at[chunk],
            device_id={"blk": partner}, device_id_type=MESH,
        )

    def up_copy(chunk, target):
        return pltpu.make_async_remote_copy(
            src_ref=stage_up.at[chunk, target], dst_ref=from_below.at[chunk, target],
            send_sem=up_send.at[chunk, target], recv_sem=up_recv.at[chunk, target],
            device_id={"blk": me + 2}, device_id_type=MESH,
        )

    def down_copy(chunk, target):
        return pltpu.make_async_remote_copy(
            src_ref=stage_down.at[chunk, target], dst_ref=from_above.at[chunk, target],
            send_sem=down_send.at[chunk, target], recv_sem=down_recv.at[chunk, target],
            device_id={"blk": me - 2}, device_id_type=MESH,
        )

    @pl.when(step == 0)
    def _():
        barrier = pltpu.get_barrier_semaphore()
        pl.semaphore_signal(barrier, inc=1, device_id={"blk": partner}, device_id_type=MESH)

        @pl.when(has_below)
        def _():
            pl.semaphore_signal(barrier, inc=1, device_id={"blk": me - 2}, device_id_type=MESH)

        @pl.when(has_above)
        def _():
            pl.semaphore_signal(barrier, inc=1, device_id={"blk": me + 2}, device_id_type=MESH)

        pl.semaphore_wait(
            barrier, 1 + jnp.where(has_below, 1, 0) + jnp.where(has_above, 1, 0)
        )

    @pl.when(step < chunks)
    def _():
        top, rest = split(sky_ref[0])
        both = jnp.dot(modes_ref[...], top, preferred_element_type=jnp.float32)
        low = jnp.dot(modes_ref[: 2 * half], rest, preferred_element_type=jnp.float32)
        share = both[: 2 * half] + both[2 * half :] + low
        for target in range(chips):
            for buffer, start in ((own, target * count), (give, half + target * count)):
                buffer[step, target] = jnp.concatenate(
                    [
                        share[start : start + count, fold * folded : (fold + 1) * folded]
                        for fold in range(folds)
                    ],
                    axis=0,
                )
        pair_copy(step).start()

    paired = step - 1

    @pl.when((paired >= 0) & (paired < chunks))
    def _():
        pair_copy(paired).wait_recv()
        own[paired] += taken[paired]

    rising = step - 1 - place

    @pl.when((rising >= 0) & (rising < chunks))
    def _():
        for target in range(chips - 1, -1, -1):
            @pl.when(has_below & (target >= place))
            def _():
                up_copy(rising, target).wait_recv()

            @pl.when(has_below & (target > place))
            def _():
                stage_up[rising, target] = (
                    own[rising, target] + from_below[rising, target].astype(jnp.float32)
                ).astype(wire)

            @pl.when((place == 0) & (target > place))
            def _():
                stage_up[rising, target] = own[rising, target].astype(wire)

            @pl.when(target > place)
            def _():
                up_copy(rising, target).start()

    falling = step - chips + place

    @pl.when((falling >= 0) & (falling < chunks))
    def _():
        for target in range(chips):
            @pl.when(has_above & (target <= place))
            def _():
                down_copy(falling, target).wait_recv()

            @pl.when(has_above & (target < place))
            def _():
                stage_down[falling, target] = (
                    own[falling, target] + from_above[falling, target].astype(jnp.float32)
                ).astype(wire)

            @pl.when((place == chips - 1) & (target < place))
            def _():
                stage_down[falling, target] = own[falling, target].astype(wire)

            @pl.when(target < place)
            def _():
                down_copy(falling, target).start()

    ready = step - 1 - jnp.maximum(place, chips - 1 - place)

    @pl.when((ready >= 0) & (ready < chunks))
    def _():
        out_ref[ready] = own[ready, place]

        @pl.when(has_below)
        def _():
            out_ref[ready] += from_below[ready, place].astype(jnp.float32)

        @pl.when(has_above)
        def _():
            out_ref[ready] += from_above[ready, place].astype(jnp.float32)

    @pl.when(step == chunks + chips - 1)
    def _():
        def drain(chunk, carry):
            pair_copy(chunk).wait_send()
            for target in range(chips):
                @pl.when(target > place)
                def _():
                    up_copy(chunk, target).wait_send()

                @pl.when(target < place)
                def _():
                    down_copy(chunk, target).wait_send()

            return carry

        lax.fori_loop(0, chunks, drain, 0)


def project(sky_data, local_modes):
    channels, length = sky_data.shape[1:]
    modes = local_modes.shape[1]
    chips = lax.axis_size("blk") // 2
    count = modes // (2 * chips)
    folds = max(16 // count, 1)
    width = 2048
    chunks = length // width
    core = lax.axis_index("blk") % 2
    by_core = local_modes.reshape(channels, chips, 2, count)
    mine = lax.dynamic_index_in_dim(by_core, core, 2, keepdims=False)
    others = lax.dynamic_index_in_dim(by_core, 1 - core, 2, keepdims=False)
    ordered = jnp.concatenate([mine.reshape(channels, -1), others.reshape(channels, -1)], axis=1)
    wide = jnp.concatenate(split(ordered), axis=1).T
    wire = jnp.bfloat16 if chips <= 4 else jnp.float32
    block = (chunks, chips, folds * count, width // folds)
    summed = pl.pallas_call(
        functools.partial(scatter_kernel, chips, chunks, wire),
        grid=(chunks + chips,),
        in_specs=[
            pl.BlockSpec(wide.shape, lambda i: (0, 0)),
            pl.BlockSpec((1, channels, width), lambda i: (0, 0, jnp.minimum(i, chunks - 1))),
        ],
        out_specs=pl.BlockSpec((chunks,) + block[2:], lambda i: (0, 0, 0)),
        out_shape=jax.ShapeDtypeStruct((chunks,) + block[2:], jnp.float32),
        scratch_shapes=[pltpu.VMEM(block, jnp.float32)] * 3
        + [pltpu.VMEM(block, wire)] * 4
        + [pltpu.SemaphoreType.DMA((chunks,))] * 2
        + [pltpu.SemaphoreType.DMA((chunks, chips))] * 4,
        compiler_params=pltpu.CompilerParams(
            collective_id=0, has_side_effects=True, vmem_limit_bytes=56 * 2**20
        ),
    )(wide, sky_data)
    summed = summed.reshape(chunks, folds, count, width // folds)
    return jnp.transpose(summed, (2, 0, 1, 3)).reshape(count, length)


def power_kernel(rounds, here_ref, out_ref, stage, taken, send, recv):
    me = lax.axis_index("dish")
    middle = here_ref.shape[1] // 2

    def peer(bit):
        return me + (1 << bit) - 2 * ((me // (1 << bit)) % 2) * (1 << bit)

    barrier = pltpu.get_barrier_semaphore()
    for bit in range(rounds):
        pl.semaphore_signal(barrier, inc=1, device_id={"dish": peer(bit)}, device_id_type=MESH)
    pl.semaphore_wait(barrier, rounds)
    out_ref[...] = here_ref[...]
    for turn in range(rounds):
        copies = []
        for side in range(2):
            bit = turn if side == 0 else rounds - 1 - turn
            rows = pl.ds(side * middle, middle)
            stage[turn, side] = out_ref[:, rows, :].astype(stage.dtype)
            copy = pltpu.make_async_remote_copy(
                src_ref=stage.at[turn, side], dst_ref=taken.at[turn, side],
                send_sem=send.at[turn, side], recv_sem=recv.at[turn, side],
                device_id={"dish": peer(bit)}, device_id_type=MESH,
            )
            copy.start()
            copies.append((copy, rows))
        for side, (copy, rows) in enumerate(copies):
            copy.wait()
            out_ref[:, rows, :] += taken[turn, side].astype(jnp.float32)


def sum_over_dishes(power_here):
    dishes = lax.axis_size("dish")
    rounds = dishes.bit_length() - 1
    if rounds == 0 or dishes != 1 << rounds:
        return lax.psum(power_here, "dish")
    count, rows, columns = power_here.shape
    half = (rounds, 2, count, rows // 2, columns)
    return pl.pallas_call(
        functools.partial(power_kernel, rounds),
        in_specs=[pl.BlockSpec(memory_space=pltpu.VMEM)],
        out_specs=pl.BlockSpec(memory_space=pltpu.VMEM),
        out_shape=jax.ShapeDtypeStruct(power_here.shape, jnp.float32),
        scratch_shapes=[pltpu.VMEM(half, jnp.bfloat16)] * 2
        + [pltpu.SemaphoreType.DMA((rounds, 2))] * 2,
        compiler_params=pltpu.CompilerParams(
            collective_id=1, has_side_effects=True, vmem_limit_bytes=32 * 2**20
        ),
    )(power_here)


def clean_kernel(modes_ref, sky_ref, signal_ref, out_ref):
    signal = signal_ref[...]
    fitted = jnp.dot(
        modes_ref[...],
        jnp.concatenate([signal, signal], axis=0),
        preferred_element_type=jnp.float32,
    )
    out_ref[0] = (sky_ref[0] - fitted).astype(jnp.bfloat16)


def body(sky_data, eigenmodes, noise_power):
    channels, length = sky_data.shape[1:]
    count = eigenmodes.shape[1]
    width = min(2048, length)
    position = lax.axis_index("blk")
    local_modes = lax.dynamic_slice_in_dim(eigenmodes, position * channels, channels, 0)
    top, rest = split(local_modes)
    wide = jnp.concatenate([top, rest], axis=1)
    signal = wiener(project(sky_data, local_modes)[None], noise_power)
    everyone = lax.all_gather(signal[0].astype(jnp.bfloat16), "blk", axis=0, tiled=True)
    cleaned = pl.pallas_call(
        clean_kernel,
        grid=(length // width,),
        in_specs=[
            pl.BlockSpec((channels, 2 * count), lambda i: (0, 0)),
            pl.BlockSpec((1, channels, width), lambda i: (0, 0, i)),
            pl.BlockSpec((count, width), lambda i: (0, i)),
        ],
        out_specs=pl.BlockSpec((1, channels, width), lambda i: (0, 0, i)),
        out_shape=jax.ShapeDtypeStruct(sky_data.shape, jnp.bfloat16),
        compiler_params=pltpu.CompilerParams(vmem_limit_bytes=40 * 2**20),
    )(wide, sky_data, everyone)
    return (cleaned, signal)


def solution(mesh):
    return jax.shard_map(
        body,
        mesh=mesh,
        in_specs=(P("dish", "blk", None), P(), P("blk", None)),
        out_specs=(P("dish", "blk", None), P("dish", "blk", None)),
        check_vma=False,
    )
```

```python
import functools
import math

import jax
import jax.numpy as jnp
from jax import lax
from jax.experimental import pallas as pl
from jax.experimental.pallas import tpu as pltpu
from jax.sharding import PartitionSpec as P

highest = lax.Precision.HIGH


def dft_table(length):
    index = jnp.arange(length, dtype=jnp.int32)
    phase = (index[:, None] * index[None, :] % length).astype(jnp.float32) * (
        2.0 * math.pi / length
    )
    return (jnp.cos(phase), jnp.sin(phase))


def twist_table(rows_count, cols_count):
    total = rows_count * cols_count
    first = jnp.arange(rows_count, dtype=jnp.int32)
    second = jnp.arange(cols_count, dtype=jnp.int32)
    phase = (first[:, None] * second[None, :] % total).astype(jnp.float32) * (2.0 * math.pi / total)
    return (jnp.cos(phase), jnp.sin(phase))


def forward(series, tables):
    col_cos, col_sin, row_cos, row_sin, twist_cos, twist_sin = tables
    batch_count, length = series.shape
    grid = series.reshape(batch_count, length // 128, 128)
    inner_real = jnp.einsum("bqp,qk->bpk", grid, col_cos, precision=highest)
    inner_imag = -jnp.einsum("bqp,qk->bpk", grid, col_sin, precision=highest)
    turned_real = inner_real * twist_cos + inner_imag * twist_sin
    turned_imag = inner_imag * twist_cos - inner_real * twist_sin
    spec_real = jnp.einsum("kp,bpj->bkj", row_cos, turned_real, precision=highest) + jnp.einsum(
        "kp,bpj->bkj", row_sin, turned_imag, precision=highest
    )
    spec_imag = jnp.einsum("kp,bpj->bkj", row_cos, turned_imag, precision=highest) - jnp.einsum(
        "kp,bpj->bkj", row_sin, turned_real, precision=highest
    )
    return (spec_real, spec_imag)


def inverse(held_real, held_imag, tables, length):
    col_cos, col_sin, row_cos, row_sin, twist_cos, twist_sin = tables
    outer_real = jnp.einsum("pk,bkj->bpj", row_cos, held_real, precision=highest) - jnp.einsum(
        "pk,bkj->bpj", row_sin, held_imag, precision=highest
    )
    outer_imag = jnp.einsum("pk,bkj->bpj", row_cos, held_imag, precision=highest) + jnp.einsum(
        "pk,bkj->bpj", row_sin, held_real, precision=highest
    )
    back_real = outer_real * twist_cos - outer_imag * twist_sin
    back_imag = outer_real * twist_sin + outer_imag * twist_cos
    series = jnp.einsum("qk,bpk->bqp", col_cos, back_real, precision=highest) - jnp.einsum(
        "qk,bpk->bqp", col_sin, back_imag, precision=highest
    )
    return (series / length).reshape(held_real.shape[0], length)


def wiener(amplitude, noise_power):
    dish_local = amplitude.shape[0]
    owned_modes = amplitude.shape[1]
    length = amplitude.shape[2]
    columns = length // 128
    col_cos, col_sin = dft_table(columns)
    row_cos, row_sin = dft_table(128)
    twist_cos, twist_sin = twist_table(128, columns)
    tables = (col_cos, col_sin, row_cos, row_sin, twist_cos, twist_sin)
    spec_real, spec_imag = forward(amplitude.reshape(dish_local * owned_modes, length), tables)
    squared = spec_real * spec_real + spec_imag * spec_imag
    power_here = jnp.sum(squared.reshape(dish_local, owned_modes, 128, columns), axis=0)
    power_total = sum_over_dishes(power_here)
    power = power_total / float(dish_local * lax.axis_size("dish") * length)
    gain = power / (power + noise_power.reshape(owned_modes, 128, columns))
    gain_rows = gain[None].reshape(dish_local * owned_modes, 128, columns)
    signal = inverse(spec_real * gain_rows, spec_imag * gain_rows, tables, length)
    return signal.reshape(dish_local, owned_modes, length)


def split(value):
    top = value.astype(jnp.bfloat16)
    return top, (value - top.astype(jnp.float32)).astype(jnp.bfloat16)


def split_rounded(value):
    top = lax.reduce_precision(value, 8, 7)
    return top.astype(jnp.bfloat16), (value - top).astype(jnp.bfloat16)


MESH = pl.DeviceIdType.MESH
AHEAD = 2


def scatter_kernel(
    chips, chunks, wire, modes_ref, sky_ref, out_ref,
    own, give, taken, stage_up, stage_down, from_below, from_above,
    pair_send, pair_recv, up_send, up_recv, down_send, down_recv,
):
    step = pl.program_id(0)
    me = lax.axis_index("blk")
    place = me // 2
    partner = me + 1 - 2 * (me % 2)
    has_below = place > 0
    has_above = place < chips - 1
    half = modes_ref.shape[0] // 4
    count = half // chips
    folded = out_ref.shape[2]
    folds = out_ref.shape[1] // count

    def pair_copy(chunk):
        return pltpu.make_async_remote_copy(
            src_ref=give.at[chunk], dst_ref=taken.at[chunk],
            send_sem=pair_send.at[chunk], recv_sem=pair_recv.at[chunk],
            device_id={"blk": partner}, device_id_type=MESH,
        )

    def up_copy(chunk, target):
        return pltpu.make_async_remote_copy(
            src_ref=stage_up.at[chunk, target], dst_ref=from_below.at[chunk, target],
            send_sem=up_send.at[chunk, target], recv_sem=up_recv.at[chunk, target],
            device_id={"blk": me + 2}, device_id_type=MESH,
        )

    def down_copy(chunk, target):
        return pltpu.make_async_remote_copy(
            src_ref=stage_down.at[chunk, target], dst_ref=from_above.at[chunk, target],
            send_sem=down_send.at[chunk, target], recv_sem=down_recv.at[chunk, target],
            device_id={"blk": me - 2}, device_id_type=MESH,
        )

    @pl.when(step == 0)
    def _():
        barrier = pltpu.get_barrier_semaphore()
        pl.semaphore_signal(barrier, inc=1, device_id={"blk": partner}, device_id_type=MESH)

        @pl.when(has_below)
        def _():
            pl.semaphore_signal(barrier, inc=1, device_id={"blk": me - 2}, device_id_type=MESH)

        @pl.when(has_above)
        def _():
            pl.semaphore_signal(barrier, inc=1, device_id={"blk": me + 2}, device_id_type=MESH)

        pl.semaphore_wait(
            barrier, 1 + jnp.where(has_below, 1, 0) + jnp.where(has_above, 1, 0)
        )

    @pl.when(step < chunks)
    def _():
        top, rest = split(sky_ref[0])
        both = jnp.dot(modes_ref[...], top, preferred_element_type=jnp.float32)
        low = jnp.dot(modes_ref[: 2 * half], rest, preferred_element_type=jnp.float32)
        share = both[: 2 * half] + both[2 * half :] + low
        for target in range(chips):
            for buffer, start in ((own, target * count), (give, half + target * count)):
                buffer[step, target] = jnp.concatenate(
                    [
                        share[start : start + count, fold * folded : (fold + 1) * folded]
                        for fold in range(folds)
                    ],
                    axis=0,
                )
        pair_copy(step).start()

    paired = step - 1

    @pl.when((paired >= 0) & (paired < chunks))
    def _():
        pair_copy(paired).wait_recv()
        own[paired] += taken[paired]

    rising = step - 1 - place

    @pl.when((rising >= 0) & (rising < chunks))
    def _():
        @pl.when(rising >= AHEAD)
        def _():
            for target in range(1, chips):
                @pl.when(target > place)
                def _():
                    up_copy(rising - AHEAD, target).wait_send()

        for target in range(chips - 1, -1, -1):
            @pl.when(has_below & (target >= place))
            def _():
                up_copy(rising, target).wait_recv()

            @pl.when(has_below & (target > place))
            def _():
                stage_up[rising, target] = (
                    own[rising, target] + from_below[rising, target].astype(jnp.float32)
                ).astype(wire)

            @pl.when((place == 0) & (target > place))
            def _():
                stage_up[rising, target] = own[rising, target].astype(wire)

            @pl.when(target > place)
            def _():
                up_copy(rising, target).start()

    falling = step - chips + place

    @pl.when((falling >= 0) & (falling < chunks))
    def _():
        @pl.when(falling >= AHEAD)
        def _():
            for target in range(chips - 1):
                @pl.when(target < place)
                def _():
                    down_copy(falling - AHEAD, target).wait_send()

        for target in range(chips):
            @pl.when(has_above & (target <= place))
            def _():
                down_copy(falling, target).wait_recv()

            @pl.when(has_above & (target < place))
            def _():
                stage_down[falling, target] = (
                    own[falling, target] + from_above[falling, target].astype(jnp.float32)
                ).astype(wire)

            @pl.when((place == chips - 1) & (target < place))
            def _():
                stage_down[falling, target] = own[falling, target].astype(wire)

            @pl.when(target < place)
            def _():
                down_copy(falling, target).start()

    ready = step - 1 - jnp.maximum(place, chips - 1 - place)

    @pl.when((ready >= 0) & (ready < chunks))
    def _():
        out_ref[ready] = own[ready, place]

        @pl.when(has_below)
        def _():
            out_ref[ready] += from_below[ready, place].astype(jnp.float32)

        @pl.when(has_above)
        def _():
            out_ref[ready] += from_above[ready, place].astype(jnp.float32)

    @pl.when(step == chunks + chips - 1)
    def _():
        def drain(chunk, carry):
            pair_copy(chunk).wait_send()
            return carry

        def drain_line(chunk, carry):
            for target in range(chips):
                @pl.when(target > place)
                def _():
                    up_copy(chunk, target).wait_send()

                @pl.when(target < place)
                def _():
                    down_copy(chunk, target).wait_send()

            return carry

        lax.fori_loop(0, chunks, drain, 0)
        lax.fori_loop(chunks - AHEAD, chunks, drain_line, 0)


def project(sky_data, local_modes):
    channels, length = sky_data.shape[1:]
    modes = local_modes.shape[1]
    chips = lax.axis_size("blk") // 2
    count = modes // (2 * chips)
    folds = max(16 // count, 1)
    width = 2048
    chunks = length // width
    core = lax.axis_index("blk") % 2
    by_core = local_modes.reshape(channels, chips, 2, count)
    mine = lax.dynamic_index_in_dim(by_core, core, 2, keepdims=False)
    others = lax.dynamic_index_in_dim(by_core, 1 - core, 2, keepdims=False)
    ordered = jnp.concatenate([mine.reshape(channels, -1), others.reshape(channels, -1)], axis=1)
    wide = jnp.concatenate(split_rounded(ordered), axis=1).T
    wire = jnp.bfloat16 if chips <= 4 else jnp.float32
    block = (chunks, chips, folds * count, width // folds)
    summed = pl.pallas_call(
        functools.partial(scatter_kernel, chips, chunks, wire),
        grid=(chunks + chips,),
        in_specs=[
            pl.BlockSpec(wide.shape, lambda i: (0, 0)),
            pl.BlockSpec((1, channels, width), lambda i: (0, 0, jnp.minimum(i, chunks - 1))),
        ],
        out_specs=pl.BlockSpec((chunks,) + block[2:], lambda i: (0, 0, 0)),
        out_shape=jax.ShapeDtypeStruct((chunks,) + block[2:], jnp.float32),
        scratch_shapes=[pltpu.VMEM(block, jnp.float32)] * 3
        + [pltpu.VMEM(block, wire)] * 4
        + [pltpu.SemaphoreType.DMA((chunks,))] * 2
        + [pltpu.SemaphoreType.DMA((chunks, chips))] * 4,
        compiler_params=pltpu.CompilerParams(
            collective_id=0, has_side_effects=True, vmem_limit_bytes=56 * 2**20
        ),
    )(wide, sky_data)
    summed = summed.reshape(chunks, folds, count, width // folds)
    return jnp.transpose(summed, (2, 0, 1, 3)).reshape(count, length)


def power_kernel(rounds, here_ref, out_ref, stage, taken, send, recv):
    me = lax.axis_index("dish")
    middle = here_ref.shape[1] // 2

    def peer(bit):
        return me + (1 << bit) - 2 * ((me // (1 << bit)) % 2) * (1 << bit)

    barrier = pltpu.get_barrier_semaphore()
    for bit in range(rounds):
        pl.semaphore_signal(barrier, inc=1, device_id={"dish": peer(bit)}, device_id_type=MESH)
    pl.semaphore_wait(barrier, rounds)
    out_ref[...] = here_ref[...]
    for turn in range(rounds):
        copies = []
        for side in range(2):
            bit = turn if side == 0 else rounds - 1 - turn
            rows = pl.ds(side * middle, middle)
            stage[turn, side] = out_ref[:, rows, :].astype(stage.dtype)
            copy = pltpu.make_async_remote_copy(
                src_ref=stage.at[turn, side], dst_ref=taken.at[turn, side],
                send_sem=send.at[turn, side], recv_sem=recv.at[turn, side],
                device_id={"dish": peer(bit)}, device_id_type=MESH,
            )
            copy.start()
            copies.append((copy, rows))
        for side, (copy, rows) in enumerate(copies):
            copy.wait()
            out_ref[:, rows, :] += taken[turn, side].astype(jnp.float32)


def sum_over_dishes(power_here):
    dishes = lax.axis_size("dish")
    rounds = dishes.bit_length() - 1
    if rounds == 0 or dishes != 1 << rounds:
        return lax.psum(power_here, "dish")
    count, rows, columns = power_here.shape
    half = (rounds, 2, count, rows // 2, columns)
    return pl.pallas_call(
        functools.partial(power_kernel, rounds),
        in_specs=[pl.BlockSpec(memory_space=pltpu.VMEM)],
        out_specs=pl.BlockSpec(memory_space=pltpu.VMEM),
        out_shape=jax.ShapeDtypeStruct(power_here.shape, jnp.float32),
        scratch_shapes=[pltpu.VMEM(half, jnp.bfloat16)] * 2
        + [pltpu.SemaphoreType.DMA((rounds, 2))] * 2,
        compiler_params=pltpu.CompilerParams(
            collective_id=1, has_side_effects=True, vmem_limit_bytes=32 * 2**20
        ),
    )(power_here)


def clean_kernel(modes_ref, sky_ref, signal_ref, *rest):
    out_ref = rest[-1]
    tile = 256
    for start in range(0, out_ref.shape[2], tile):
        columns = slice(start, start + tile)
        signal = signal_ref[:, columns]
        fitted = jnp.dot(
            modes_ref[...],
            jnp.concatenate([signal, signal], axis=0),
            preferred_element_type=jnp.float32,
        )
        out_ref[0, :, columns] = (sky_ref[0, :, columns] - fitted).astype(jnp.bfloat16)


def clean(sky_data, wide, signal, first, before):
    channels = sky_data.shape[1]
    count, length = signal.shape
    width = 2048
    skip = first // width
    held = [] if before is None else [before]
    return pl.pallas_call(
        clean_kernel,
        grid=(length // width,),
        in_specs=[
            pl.BlockSpec(wide.shape, lambda i: (0, 0)),
            pl.BlockSpec((1, channels, width), lambda i: (0, 0, i + skip)),
            pl.BlockSpec((count, width), lambda i: (0, i)),
        ]
        + [pl.BlockSpec(memory_space=pl.ANY)] * len(held),
        out_specs=pl.BlockSpec((1, channels, width), lambda i: (0, 0, i + skip)),
        out_shape=jax.ShapeDtypeStruct(sky_data.shape, jnp.bfloat16),
        input_output_aliases={3: 0} if held else {},
        cost_estimate=pl.CostEstimate(
            flops=4 * channels * count * length,
            bytes_accessed=6 * channels * length,
            transcendentals=0,
        ),
        compiler_params=pltpu.CompilerParams(vmem_limit_bytes=40 * 2**20),
    )(wide, sky_data, signal, *held)


def body(sky_data, eigenmodes, noise_power):
    channels, length = sky_data.shape[1:]
    position = lax.axis_index("blk")
    local_modes = lax.dynamic_slice_in_dim(eigenmodes, position * channels, channels, 0)
    top, rest = split_rounded(local_modes)
    wide = jnp.concatenate([top, rest], axis=1)
    signal = wiener(project(sky_data, local_modes)[None], noise_power)
    narrow = signal[0].astype(jnp.bfloat16)
    cut = length // 4 * 3
    early = lax.all_gather(narrow[:, :cut], "blk", axis=0, tiled=True)
    late = lax.all_gather(narrow[:, cut:], "blk", axis=0, tiled=True)
    cleaned = clean(sky_data, wide, early, 0, None)
    cleaned = clean(sky_data, wide, late, cut, cleaned)
    return (cleaned, signal)


def solution(mesh):
    return jax.shard_map(
        body,
        mesh=mesh,
        in_specs=(P("dish", "blk", None), P(), P("blk", None)),
        out_specs=(P("dish", "blk", None), P("dish", "blk", None)),
        check_vma=False,
    )
```
